256 devices in a mesh: sta: 64 (over y, x, z_hi, core), win: 4 (over z_lo).
Axes of the slice: x: 4, y: 4, z: 8 (z_hi: 2, z_lo: 4; z = z_hi * 4 + z_lo), core: 2. Of those that a mesh axis runs over, the one named last changes fastest.
Arguments:
- records: bfloat16 [16, 4096, 2048], P('win', 'sta'), may hold values from -6 to 6
- record_block: int32 [16, 4096, 1], P('win', 'sta'), may hold values from 0 to 63; in each aligned block of 64 rows (0 to 63, 64 to 127, ..., all dimensions but the last counted through in order) at most 2 rows name the same one
- record_station: int32 [16, 4096], P('win', 'sta'), may hold values from 0 to 31
- quality: int32 [16, 4096], P('win', 'sta'), may hold values 0 or 1
Outputs:
- correlation: bfloat16 [2, 32, 2048, 2048], P(None, 'win', 'sta')
The draws below stay inside these ranges and needn't reach their ends.
Inputs may be any that keep to these rules, and one draw needn't show every extreme that they name: `record_block`: in each hour, of the 64 records that one index of sta holds, at most 2 name one station block, and some block is named by exactly 2 of them.
All inputs are finite; a program needn't handle non-finite values. No bound on the sum of `quality` on one device may be relied on, other than what follows from the above.
Results may differ from the reference program's by a relative error of at most 0.0071.
Values may be sent and summed in bfloat16 or wider, within the bound.
A program may use at most 128 MiB of HBM per device.

```python
import math
import jax
import jax.numpy as jnp
import numpy as np
from jax import lax

FREQ = 1024
LAGS = 2048
SMOOTH = 32
ROUNDS = 2
STA_DEV = 32
REC_DEV = 64
CAP = 2
HOURS = 16
RECS = 4096
N_STA = 64


def touch_ends(result, key, least, high):
    shape = result.shape
    place = [jax.random.randint(jax.random.fold_in(key, axis), (), 0, shape[axis]) for axis in range(len(shape))]
    result = result.at[tuple(place)].set(least)
    longest = shape.index(max(shape))
    place[longest] = (place[longest] + 1) % shape[longest]
    return result.at[tuple(place)].set(high)


def level_of(own_key, dims, cuts, smallest, top_value):
    factor_of = 1.0
    for position, parts in cuts:
        heights = jax.random.uniform(jax.random.fold_in(jax.random.fold_in(own_key, 6), position), (parts,), jnp.float32, smallest / len(cuts), top_value / len(cuts))
        factor_of = factor_of * jnp.repeat(jnp.exp(heights), dims[position] // parts).reshape((-1,) + (1,) * (len(dims) - 1 - position))
    return factor_of


def routed_block(rng, own, number, rows, number_of, top, bound, skew):
    ranking = jax.random.permutation(rng, number_of)
    crowded, usual = load_shares(number_of, rows * top, bound, skew, True), load_shares(number_of, rows * top, bound, skew, False)
    places = jnp.arange(number_of)

    def named(lengths, turn):
        used = int((lengths > 0).sum())
        fixed = max(1, used // 4)
        moved = fixed + (places - fixed + turn * (used - fixed)) % max(1, number_of - fixed)
        return jnp.zeros((number_of,), jnp.int32).at[ranking[jnp.where(places < fixed, places, moved)]].set(jnp.asarray(lengths, jnp.int32))

    lengths = jnp.where(number % 4 == 0, named(crowded, number // 4), named(usual, number - number // 4 - 1))
    mixed = jax.random.permutation(jax.random.fold_in(own, 3), number_of)
    donor, taker = mixed[0:number_of // 2 * 2:2], mixed[1:number_of // 2 * 2:2]
    room = jnp.minimum(lengths[donor] - 1, bound - lengths[taker]) // 2
    room = jnp.where((donor == ranking[0]) | (taker == ranking[0]) | (lengths[taker] == 0), 0, jnp.maximum(room, 0))
    moved = jax.random.randint(jax.random.fold_in(own, 4), (number_of // 2,), 0, 1 << 20) % (room + 1)
    lengths = lengths.at[donor].add(-moved).at[taker].add(moved)
    items = jnp.searchsorted(jnp.cumsum(lengths), jnp.arange(rows * top), side="right").astype(jnp.int32)
    listing = items.reshape(top, rows).T
    listing = listing[jax.random.permutation(jax.random.fold_in(own, 1), rows)]
    turn = jax.random.randint(jax.random.fold_in(own, 2), (rows, 1), 0, top)
    return jnp.take_along_axis(listing, (jnp.arange(top)[None, :] + turn) % top, axis=1)


def load_shares(count, total, limit, skew, full):
    loads = [(1 << 20) // math.isqrt(standing ** skew) + 1 for standing in range(1, count + 1)]
    largest = limit if full else min(limit, max(-(-total // count), total * loads[0] // sum(loads)))
    least = 1 if total - largest >= count - 1 else 0
    given, rest = [largest] + [least] * (count - 1), total - largest - least * (count - 1)
    while rest > 0:
        free = [i for i in range(1, count) if given[i] < largest] or [i for i in range(1, count) if given[i] < limit]
        mass, budget = sum([loads[i] for i in free]), rest
        for i in free:
            extra = min(limit - given[i], max(1, budget * loads[i] // mass), rest)
            given[i] = given[i] + extra
            rest = rest - extra
    return np.array(given)


def scatter_about(stream_key, dims, width, limit, pieces=(), kind=jnp.bfloat16):
    drawn = width * jax.random.normal(stream_key, dims, jnp.float32)
    if pieces:
        drawn = drawn * level_of(stream_key, dims, pieces, -0.22, 0.18)
    return jnp.clip(drawn, -limit, limit).astype(kind)


def setup_inputs(seed: int = 0) -> dict:
    streams_of = jax.random.split(jax.random.key(seed), 5)
    records = scatter_about(streams_of[0], (HOURS, RECS, 2 * FREQ), 1.0, 6.0, ((0, 4), (1, 64)))
    record_block_keys = jax.random.split(jax.random.fold_in(streams_of[1], 1), HOURS * RECS // REC_DEV)
    record_block_turns = jax.random.permutation(jax.random.fold_in(streams_of[1], 3), HOURS * RECS // REC_DEV)
    record_block = jax.vmap(lambda own, number: routed_block(jax.random.fold_in(streams_of[1], 2), own, number, REC_DEV, N_STA, 1, CAP, 2))(record_block_keys, record_block_turns).reshape((HOURS, RECS, 1))
    record_station = touch_ends(jax.random.randint(streams_of[2], (HOURS, RECS), 0, STA_DEV), jax.random.fold_in(streams_of[2], 1), 0, STA_DEV - 1).astype(jnp.int32)
    quality = touch_ends((jax.random.randint(streams_of[3], (HOURS, RECS), 0, 4) < 3).astype(jnp.int32), jax.random.fold_in(streams_of[3], 1), 0, 1)
    return {"records": records, "record_block": record_block, "record_station": record_station, "quality": quality}


epsilon = 1e-05

def band_table(freq_bins, smooth):
    row_index = lax.broadcasted_iota(jnp.int32, (freq_bins, freq_bins), 0)
    col_index = lax.broadcasted_iota(jnp.int32, (freq_bins, freq_bins), 1)
    distance = (row_index - col_index) % freq_bins
    inside = jnp.minimum(distance, freq_bins - distance) <= smooth
    return inside.astype(jnp.float32) / (2 * smooth + 1)

def lag_table(freq_bins, lag_count, hour_count):
    bin_index = lax.broadcasted_iota(jnp.int32, (freq_bins, lag_count), 0) + 1
    lag_offset = lax.broadcasted_iota(jnp.int32, (freq_bins, lag_count), 1) - lag_count // 2
    phase_turns = bin_index * lag_offset % (4 * freq_bins)
    radians = phase_turns.astype(jnp.float32) * (2.0 * math.pi / (4 * freq_bins))
    scaling = 1.0 / math.sqrt(2.0 * freq_bins * hour_count)
    joined = jnp.concatenate([jnp.cos(radians), -jnp.sin(radians)], axis=0) * scaling
    return joined.astype(jnp.bfloat16)

def whiten(summed, smooth):
    freq_bins = summed.shape[-1] // 2
    real_part = summed[..., :freq_bins]
    imag_part = summed[..., freq_bins:]
    magnitude = jnp.sqrt(real_part * real_part + imag_part * imag_part)
    level_mean = jnp.dot(magnitude, band_table(freq_bins, smooth), precision=lax.Precision.HIGHEST)
    divisor = level_mean + epsilon
    return jnp.concatenate([real_part / divisor, imag_part / divisor], axis=-1).astype(jnp.bfloat16)

def outer_sum(left_part, right_part):
    return jnp.einsum('htf,hsf->tsf', left_part.astype(jnp.float32), right_part.astype(jnp.float32), precision=lax.Precision.HIGHEST)

def cross_spectra(partner, own_block):
    freq_bins = own_block.shape[-1] // 2
    partner_real = partner[..., :freq_bins]
    partner_imag = partner[..., freq_bins:]
    own_real = own_block[..., :freq_bins]
    own_imag = own_block[..., freq_bins:]
    real_sum = outer_sum(partner_real, own_real) + outer_sum(partner_imag, own_imag)
    imag_sum = outer_sum(partner_real, own_imag) - outer_sum(partner_imag, own_real)
    return jnp.concatenate([real_sum, imag_sum], axis=-1)

def reference(records, record_block, record_station, quality):
    stations = STA_DEV * N_STA
    station_id = (record_block[:, :, 0] * STA_DEV + record_station).astype(jnp.int32)

    def one_hour(hour_items):
        hour_rows, owners, passed = hour_items
        values = hour_rows.astype(jnp.float32) * passed.astype(jnp.float32)[:, None]
        summed = jax.ops.segment_sum(values, owners, num_segments=stations)
        return whiten(summed, SMOOTH)
    whitened = lax.map(one_hour, (records, station_id, quality))
    lag_weights = lag_table(FREQ, LAGS, HOURS)
    white_blocks = whitened.reshape(HOURS, N_STA, STA_DEV, 2 * FREQ)
    outputs = []
    for round_index in range(1, ROUNDS + 1):

        def one_block(block_index):
            own_block = lax.dynamic_index_in_dim(white_blocks, block_index, 1, keepdims=False)
            partner_index = ((block_index - round_index) % N_STA).astype(jnp.int32)
            partner = lax.dynamic_index_in_dim(white_blocks, partner_index, 1, keepdims=False)
            stacked = cross_spectra(partner, own_block).astype(jnp.bfloat16)
            flattened = stacked.reshape(STA_DEV * STA_DEV, 2 * FREQ)
            lagged = jnp.dot(flattened, lag_weights, preferred_element_type=jnp.float32)
            return lagged.astype(jnp.bfloat16).reshape(STA_DEV, STA_DEV, LAGS)
        per_block = lax.map(one_block, jnp.arange(N_STA, dtype=jnp.int32))
        outputs.append(jnp.transpose(per_block, (1, 0, 2, 3)).reshape(STA_DEV, stations, LAGS))
    return jnp.stack(outputs, axis=0)
```

```python
import math

import jax
import jax.numpy as jnp
import numpy as np
from jax import lax
from jax.experimental import pallas as pl
from jax.experimental.pallas import tpu as pltpu
from jax.sharding import PartitionSpec as P

MESH = pl.DeviceIdType.MESH
BINS = 1024
LAGS = 2048
SMOOTH = 32
ROUNDS = 2
EPSILON = 1e-05
HOURS_DEV = 4
RECS_DEV = 64
WIN = 4
STA = 64
PLANE = 32
PIECES = 4
PB = BINS // PIECES
PW = 2 * PB
LANES = 128

OFFSETS = sorted(
    [(dy, dx, dc) for dy in range(4) for dx in range(4) for dc in range(2)][1:],
    key=lambda t: min(t[0], 4 - t[0]) + min(t[1], 4 - t[1]),
)


def remote(src, dst, send, recv, device):
    return pltpu.make_async_remote_copy(
        src_ref=src, dst_ref=dst, send_sem=send, recv_sem=recv, device_id=device, device_id_type=MESH
    )


def kernel(
    rows, key_col, rec, cos_u, sin_u, cos_v, sin_v, out,
    sbuf, rbuf, tag_s, tag_r, assign, psum, zsend, zrecv, mag_hi, mag_lo, gath, part, part32, table, stack, acc,
    plane_send, plane_recv, tag_send, tag_recv, z_send, z_recv, g_send, g_recv, p_send, p_recv,
):
    sta, win = lax.axis_index("sta"), lax.axis_index("win")
    y, x, zh, core = sta // 16, (sta // 4) % 4, (sta // 2) % 2, sta % 2
    slot = (sta // 4) * 2 + core

    def plane_peer(offset):
        y2, x2, c2 = (y + offset[0]) % 4, (x + offset[1]) % 4, (core + offset[2]) % 2
        return (((y2 * 4 + x2) * 2 + zh) * 2 + c2, win), (y2 * 4 + x2) * 2 + c2

    z_peer = (sta + 2 - 4 * zh, win)
    win_peers = [(sta, (win + d) % WIN) for d in range(1, WIN)]

    barrier = pltpu.get_barrier_semaphore()
    greeted = [plane_peer(o)[0] for o in OFFSETS] + [z_peer] + win_peers
    greeted += [((sta + d) % STA, w2) for d in (1, 2, STA - 1, STA - 2) for w2 in range(WIN)]
    for device in greeted:
        pl.semaphore_signal(barrier, inc=1, device_id=device, device_id_type=MESH)

    count = HOURS_DEV * RECS_DEV
    hour_row = lax.broadcasted_iota(jnp.int32, (1, count), 1) // RECS_DEV
    hour_col = lax.broadcasted_iota(jnp.int32, (count, 1), 0) // RECS_DEV
    block = rows[0:1, :]
    key_r = block + hour_row * STA
    key_c = key_col[...] + hour_col * STA
    before = lax.broadcasted_iota(jnp.int32, (count, count), 0) < lax.broadcasted_iota(jnp.int32, (count, count), 1)
    rank = jnp.sum(jnp.where(before & (key_c == key_r), 1.0, 0.0), axis=0, keepdims=True).astype(jnp.int32)
    target = ((block // 4) * 2 + block % 2) * 16 + hour_row * 4 + ((block // 2) % 2) * 2 + rank
    target = jnp.where(rows[2:3, :] > 0, target, -1)
    chosen = lax.broadcasted_iota(jnp.int32, (PLANE * 16, count), 0) == target
    tags = jnp.sum(jnp.where(chosen, (rows[1:2, :] + 1).astype(jnp.float32), 0.0), axis=1, keepdims=True)
    tag_s[...] = jnp.broadcast_to(tags, (PLANE * 16, LANES)).astype(jnp.bfloat16).reshape(PLANE, 16, LANES)
    placing = jnp.where(chosen, 1.0, 0.0).astype(jnp.bfloat16)

    pl.semaphore_wait(barrier, len(greeted))

    for offset in OFFSETS:
        device, place = plane_peer(offset)
        remote(tag_s.at[place], tag_r.at[slot], tag_send, tag_recv, device).start()
    tag_r[slot] = tag_s[slot]
    for p in range(PIECES):
        for half in range(2):
            lanes = pl.ds(half * BINS + p * PB, PB)
            packed = jnp.dot(placing, rec[:, lanes], preferred_element_type=jnp.float32)
            sbuf[p, :, :, half * PB : (half + 1) * PB] = packed.astype(jnp.bfloat16).reshape(PLANE, 16, PB)
        for offset in OFFSETS:
            device, place = plane_peer(offset)
            remote(sbuf.at[p, place], rbuf.at[p, slot], plane_send.at[p], plane_recv.at[p], device).start()
        rbuf[p, slot] = sbuf[p, slot]

    for p in range(PIECES):

        @pl.loop(0, PB // 32)
        def _(i, p=p):
            u = p * (PB // 32) + i
            row = pl.multiple_of(i * 32, 32)
            for n in range(LAGS // 512):
                lanes = pl.ds(n * 512, 512)
                cu, su = cos_u[pl.ds(u, 1), lanes], sin_u[pl.ds(u, 1), lanes]
                cv, sv = cos_v[:, lanes], sin_v[:, lanes]
                table[p, pl.ds(row, 32), lanes] = (cu * cv - su * sv).astype(jnp.bfloat16)
                table[p, pl.ds(PB + row, 32), lanes] = (-(su * cv) - cu * sv).astype(jnp.bfloat16)

    spare = PLANE - 1
    remote(tag_s.at[pl.ds(0, spare)], tag_r.at[pl.ds(0, spare)], tag_send, tag_recv, z_peer).wait_recv()
    arrived = tag_r[...].astype(jnp.float32).astype(jnp.int32).reshape(PLANE * 16, LANES) - 1
    row_id = lax.broadcasted_iota(jnp.int32, (PLANE * 16, LANES), 0)
    member = ((row_id // 2 + zh) % 2) * 128 + (arrived // 8) * 32 + ((row_id // 4) % 4) * 8 + arrived % 8
    member = jnp.where(arrived >= 0, member, -1)
    lane_id = lax.broadcasted_iota(jnp.int32, (PLANE * 16, LANES), 1)
    for half in range(2):
        hit = jnp.where(member == lane_id + half * LANES, 1.0, 0.0)
        assign[half * LANES : (half + 1) * LANES, :] = hit.T.astype(jnp.bfloat16)
    for p in range(PIECES):
        remote(
            sbuf.at[p, pl.ds(0, spare)], rbuf.at[p, pl.ds(0, spare)], plane_send.at[p], plane_recv.at[p], z_peer
        ).wait_recv()
        sums = jnp.dot(assign[...], rbuf[p].reshape(PLANE * 16, PW), preferred_element_type=jnp.float32)
        psum[p] = sums[:128]
        zsend[p] = sums[128:].astype(jnp.bfloat16)
        remote(zsend.at[p], zrecv.at[p], z_send.at[p], z_recv.at[p], z_peer).start()

    def magnitude(p):
        remote(zsend.at[p], zrecv.at[p], z_send.at[p], z_recv.at[p], z_peer).wait_recv()
        summed = psum[p] + zrecv[p].astype(jnp.float32)
        psum[p] = summed
        re, im = summed[:, :PB], summed[:, PB:]
        mag = jnp.sqrt(re * re + im * im)
        high = mag.astype(jnp.bfloat16)
        mag_hi[p] = high
        mag_lo[p] = (mag - high.astype(jnp.float32)).astype(jnp.bfloat16)

    band_k = lax.broadcasted_iota(jnp.int32, (PW, PB), 0) - LANES
    band_n = lax.broadcasted_iota(jnp.int32, (PW, PB), 1)
    band = jnp.where(jnp.abs(band_k - band_n) <= SMOOTH, 1.0, 0.0).astype(jnp.bfloat16)

    def whiten(p):
        last, following = (p - 1) % PIECES, (p + 1) % PIECES
        level = jnp.zeros((128, PB), jnp.float32)
        for mag in (mag_hi, mag_lo):
            around = jnp.concatenate([mag[last, :, PB - LANES :], mag[p], mag[following, :, :LANES]], axis=1)
            level += jnp.dot(around, band, preferred_element_type=jnp.float32)
        inverse = 1.0 / (level * (1.0 / (2 * SMOOTH + 1)) + EPSILON)
        gath[p, win] = (psum[p] * jnp.concatenate([inverse, inverse], axis=1)).astype(jnp.bfloat16)
        mine = gath.at[p, win]
        for device in win_peers:
            remote(mine, mine, g_send.at[p], g_recv.at[p], device).start()
        for r in range(ROUNDS):
            for w2 in range(WIN):
                remote(
                    gath.at[p, win, pl.ds(w2 * 32, 32)], part.at[p, r, win], p_send.at[p], p_recv.at[p],
                    ((sta + r + 1) % STA, w2),
                ).start()

    magnitude(0)
    magnitude(1)
    for p in (1, 2):
        magnitude(p + 1)
        whiten(p)
    whiten(3)
    whiten(0)

    def finish(p, first):
        remote(
            gath.at[p, pl.ds(0, WIN - 1)], gath.at[p, pl.ds(0, WIN - 1)], g_send.at[p], g_recv.at[p], z_peer
        ).wait_recv()
        remote(part.at[p], part.at[p], p_send.at[p], p_recv.at[p], z_peer).wait_recv()
        part32[...] = part[p].astype(jnp.float32)

        @pl.loop(0, PB // LANES)
        def _(t):
            re = pl.ds(pl.multiple_of(t * LANES, LANES), LANES)
            im = pl.ds(pl.multiple_of(PB + t * LANES, LANES), LANES)
            for g in range(4):
                r = g // 2
                sums = [[[jnp.zeros((8, LANES), jnp.float32) for _ in range(2)] for _ in range(4)] for _ in range(4)]
                for w2 in range(WIN):
                    for pair in range(2):
                        own = []
                        for octet in range(4):
                            at = pl.ds(octet * 32 + pair * 16, 16)
                            own.append(
                                (gath[p, w2, at, re].astype(jnp.float32), gath[p, w2, at, im].astype(jnp.float32))
                            )
                        for e in range(2):
                            for jj in range(4):
                                row = (pair * 2 + e) * 8 + (g % 2) * 4 + jj
                                pr = jnp.broadcast_to(part32[r, w2, row : row + 1, re], (8, LANES))
                                pi = jnp.broadcast_to(part32[r, w2, row : row + 1, im], (8, LANES))
                                for octet in range(4):
                                    a = own[octet][0][e * 8 : e * 8 + 8]
                                    c = own[octet][1][e * 8 : e * 8 + 8]
                                    both = sums[jj][octet]
                                    both[0] = both[0] + pr * a + pi * c
                                    both[1] = both[1] + pr * c - pi * a
                for jj in range(4):
                    at = pl.ds((r * 8 + (g % 2) * 4 + jj) * 32, 32)
                    for half, lanes in enumerate((re, im)):
                        tile = jnp.concatenate([sums[jj][octet][half] for octet in range(4)], axis=0)
                        stack[at, lanes] = tile.astype(jnp.bfloat16)

        @pl.loop(0, LAGS // 512)
        def _(n):
            lanes = pl.ds(pl.multiple_of(n * 512, 512), 512)
            more = jnp.dot(stack[...], table[p, :, lanes], preferred_element_type=jnp.float32)
            if first:
                acc[:, lanes] = more
            else:
                acc[:, lanes] += more

    finish(1, True)
    for p in (2, 3, 0):
        finish(p, False)
    out[...] = acc[...].astype(jnp.bfloat16).reshape(out.shape)

    remote(tag_s.at[pl.ds(0, spare)], tag_r.at[pl.ds(0, spare)], tag_send, tag_recv, z_peer).wait_send()
    for p in range(PIECES):
        remote(
            sbuf.at[p, pl.ds(0, spare)], rbuf.at[p, pl.ds(0, spare)], plane_send.at[p], plane_recv.at[p], z_peer
        ).wait_send()
        remote(zsend.at[p], zrecv.at[p], z_send.at[p], z_recv.at[p], z_peer).wait_send()
        remote(
            gath.at[p, pl.ds(0, WIN - 1)], gath.at[p, pl.ds(0, WIN - 1)], g_send.at[p], g_recv.at[p], z_peer
        ).wait_send()
        remote(part.at[p], part.at[p], p_send.at[p], p_recv.at[p], z_peer).wait_send()


def angles(multiples):
    turns = np.outer(multiples, np.arange(LAGS) - LAGS // 2) % (4 * BINS)
    return turns * (2.0 * math.pi / (4 * BINS))


def shards(records, record_block, record_station, quality):
    hours, count, wide = records.shape
    scaling = 1.0 / math.sqrt(2.0 * BINS * hours * WIN)
    coarse, fine = angles(np.arange(BINS // 32) * 32 + 1), angles(np.arange(32))
    cos_u, sin_u = jnp.asarray(np.cos(coarse) * scaling, jnp.float32), jnp.asarray(np.sin(coarse) * scaling, jnp.float32)
    cos_v, sin_v = jnp.asarray(np.cos(fine), jnp.float32), jnp.asarray(np.sin(fine), jnp.float32)
    rows = jnp.stack([a.reshape(hours * count) for a in (record_block, record_station, quality)])
    vmem = pl.BlockSpec(memory_space=pltpu.VMEM)
    dma = pltpu.SemaphoreType.DMA
    bf16, f32 = jnp.bfloat16, jnp.float32
    return pl.pallas_call(
        kernel,
        out_shape=jax.ShapeDtypeStruct((ROUNDS, 8, 32, LAGS), bf16),
        in_specs=[vmem] * 7,
        out_specs=vmem,
        scratch_shapes=[
            pltpu.VMEM((PIECES, PLANE, 16, PW), bf16),
            pltpu.VMEM((PIECES, PLANE, 16, PW), bf16),
            pltpu.VMEM((PLANE, 16, LANES), bf16),
            pltpu.VMEM((PLANE, 16, LANES), bf16),
            pltpu.VMEM((256, PLANE * 16), bf16),
            pltpu.VMEM((PIECES, 128, PW), f32),
            pltpu.VMEM((PIECES, 128, PW), bf16),
            pltpu.VMEM((PIECES, 128, PW), bf16),
            pltpu.VMEM((PIECES, 128, PB), bf16),
            pltpu.VMEM((PIECES, 128, PB), bf16),
            pltpu.VMEM((PIECES, WIN, 128, PW), bf16),
            pltpu.VMEM((PIECES, ROUNDS, WIN, 32, PW), bf16),
            pltpu.VMEM((ROUNDS, WIN, 32, PW), f32),
            pltpu.VMEM((PIECES, PW, LAGS), bf16),
            pltpu.VMEM((512, PW), bf16),
            pltpu.VMEM((512, LAGS), f32),
            dma((PIECES,)), dma((PIECES,)), dma, dma, dma((PIECES,)), dma((PIECES,)),
            dma((PIECES,)), dma((PIECES,)), dma((PIECES,)), dma((PIECES,)),
        ],
        compiler_params=pltpu.CompilerParams(
            collective_id=0, has_side_effects=True, vmem_limit_bytes=56 * 2**20
        ),
        name="correlate",
    )(rows, record_block.reshape(hours * count, 1), records.reshape(hours * count, wide), cos_u, sin_u, cos_v, sin_v)


def solution(mesh):
    in_specs = (P("win", "sta", None), P("win", "sta", None), P("win", "sta"), P("win", "sta"))
    out_specs = P(None, "win", "sta", None)
    return jax.shard_map(shards, mesh=mesh, in_specs=in_specs, out_specs=out_specs, check_vma=False)
```

```python
import math

import jax
import jax.numpy as jnp
import numpy as np
from jax import lax
from jax.experimental import pallas as pl
from jax.experimental.pallas import tpu as pltpu
from jax.sharding import PartitionSpec as P

MESH = pl.DeviceIdType.MESH
BINS = 1024
LAGS = 2048
SMOOTH = 32
ROUNDS = 2
EPSILON = 1e-05
HOURS_DEV = 4
RECS_DEV = 64
WIN = 4
STA = 64
PLANE = 32
PIECES = 4
PB = BINS // PIECES
PW = 2 * PB
LANES = 128

def remote(src, dst, send, recv, device):
    return pltpu.make_async_remote_copy(
        src_ref=src, dst_ref=dst, send_sem=send, recv_sem=recv, device_id=device, device_id_type=MESH
    )


def kernel(
    blocks, stations, quality, rec, cos_u, sin_u, cos_v, sin_v, out,
    sbuf, xbuf, rbuf, tag_s, tag_x, tag_r, assign, psum, zsend, zrecv, mag_hi, mag_lo, gath, part, part32, table, stack, acc,
    a_send, a_recv, b_send, b_recv, t_send, t_recv, z_send, z_recv, g_send, g_recv, c_send, c_recv, x_send, x_recv,
):
    sta, win = lax.axis_index("sta"), lax.axis_index("win")
    y, x, zh, core = sta // 16, (sta // 4) % 4, (sta // 2) % 2, sta % 2

    def in_plane(y2, x2, c2):
        return (((y2 * 4 + x2) * 2 + zh) * 2 + c2, win)

    z_peer = (sta + 2 - 4 * zh, win)
    other_core = (sta + 1 - 2 * core, win)

    barrier = pltpu.get_barrier_semaphore()
    greeted = [z_peer, other_core] + [(sta, (win + d) % WIN) for d in range(1, WIN)]
    greeted += [in_plane((y + d) % 4, x, (core + dc) % 2) for d in range(1, 4) for dc in range(2)]
    greeted += [in_plane(y, (x + d) % 4, (core + dc) % 2) for d in range(1, 4) for dc in range(2)]
    greeted += [((sta + d) % STA, w2) for d in (2, STA - 2) for w2 in range(WIN)]
    for device in greeted:
        pl.semaphore_signal(barrier, inc=1, device_id=device, device_id_type=MESH)

    count = HOURS_DEV * RECS_DEV
    hour_row = lax.broadcasted_iota(jnp.int32, (1, count), 1) // RECS_DEV
    block = jnp.concatenate([blocks[h] for h in range(HOURS_DEV)], axis=1)
    station = jnp.concatenate([stations[h : h + 1, :] for h in range(HOURS_DEV)], axis=1)
    passed = jnp.concatenate([quality[h : h + 1, :] for h in range(HOURS_DEV)], axis=1)
    key = (block + hour_row * STA).astype(jnp.float32)
    from_row = lax.broadcasted_iota(jnp.int32, (count, count), 0)
    to_row = lax.broadcasted_iota(jnp.int32, (count, count), 1)
    key_col = jnp.sum(jnp.where(from_row == to_row, key, 0.0), axis=1, keepdims=True)
    earlier = (from_row < to_row) & (key_col == key)
    rank = jnp.sum(jnp.where(earlier, 1.0, 0.0), axis=0, keepdims=True).astype(jnp.int32)
    target = ((block // 4) * 2 + block % 2) * 16 + hour_row * 4 + ((block // 2) % 2) * 2 + rank
    target = jnp.where(passed > 0, target, -1)
    chosen = lax.broadcasted_iota(jnp.int32, (PLANE * 16, count), 0) == target
    tags = jnp.sum(jnp.where(chosen, (station + 1).astype(jnp.float32), 0.0), axis=1, keepdims=True)
    tag_s[...] = jnp.broadcast_to(tags, (PLANE * 16, LANES)).astype(jnp.bfloat16).reshape(tag_s.shape)
    placing = jnp.where(chosen, 1.0, 0.0).astype(jnp.bfloat16)

    pl.semaphore_wait(barrier, len(greeted))

    def spread(source, between, send, recv, x_first):
        for d in range(1, 4):
            if x_first:
                x2 = (x + d) % 4
                remote(source.at[:, x2], between.at[x], send, recv, in_plane(y, x2, core)).start()
            else:
                y2 = (y + d) % 4
                remote(source.at[y2], between.at[y], send, recv, in_plane(y2, x, core)).start()
        own = source.at[:, x] if x_first else source.at[y]
        pltpu.make_async_copy(own, between.at[x if x_first else y], recv).start()

    def deliver(between, arrived, recv, send_on, recv_on, x_first):
        pltpu.make_async_copy(between, between, recv).wait()
        for d in (1, 2, 3, 0):
            for dc in (1, 0):
                c2 = (core + dc) % 2
                if x_first:
                    y2 = (y + d) % 4
                    src, dst, device = between.at[:, y2, c2], arrived.at[y, :, core], in_plane(y2, x, c2)
                else:
                    x2 = (x + d) % 4
                    src, dst, device = between.at[:, x2, c2], arrived.at[:, x, core], in_plane(y, x2, c2)
                if d or dc:
                    remote(src, dst, send_on, recv_on, device).start()
                else:
                    pltpu.make_async_copy(src, dst, recv_on).start()

    spread(tag_s, tag_x, t_send.at[0], t_recv.at[0], True)
    for p in range(PIECES):
        for half in range(2):
            lanes = pl.ds(half * BINS + p * PB, PB)
            packed = jnp.dot(placing, rec[:, lanes], preferred_element_type=jnp.float32)
            sbuf[p, :, :, :, :, half * PB : (half + 1) * PB] = packed.astype(jnp.bfloat16).reshape(4, 4, 2, 16, PB)
        spread(sbuf.at[p], xbuf.at[p], a_send.at[p], a_recv.at[p], p % 2 == 0)
    deliver(tag_x, tag_r, t_recv.at[0], t_send.at[1], t_recv.at[1], True)

    def weigh(p):
        @pl.loop(0, PB // 32)
        def _(i):
            u = p * (PB // 32) + i
            row = pl.multiple_of(i * 32, 32)
            for n in range(LAGS // 512):
                lanes = pl.ds(n * 512, 512)
                cu, su = cos_u[pl.ds(u, 1), lanes], sin_u[pl.ds(u, 1), lanes]
                cv, sv = cos_v[:, lanes], sin_v[:, lanes]
                table[p, pl.ds(row, 32), lanes] = (cu * cv - su * sv).astype(jnp.bfloat16)
                table[p, pl.ds(PB + row, 32), lanes] = (-(su * cv) - cu * sv).astype(jnp.bfloat16)

    weigh(0)
    weigh(1)
    for p in range(PIECES):
        deliver(xbuf.at[p], rbuf.at[p], a_recv.at[p], b_send.at[p], b_recv.at[p], p % 2 == 0)
    weigh(2)
    weigh(3)

    pltpu.make_async_copy(tag_r, tag_r, t_recv.at[1]).wait()
    label = tag_r[...].astype(jnp.float32).astype(jnp.int32).reshape(PLANE * 16, LANES) - 1
    row_id = lax.broadcasted_iota(jnp.int32, (PLANE * 16, LANES), 0)
    member = ((row_id // 2 + zh) % 2) * 128 + (label // 8) * 32 + ((row_id // 4) % 4) * 8 + label % 8
    member = jnp.where(label >= 0, member, -1)
    lane_id = lax.broadcasted_iota(jnp.int32, (PLANE * 16, LANES), 1)
    for half in range(2):
        hit = jnp.where(member == lane_id + half * LANES, 1.0, 0.0)
        assign[half * LANES : (half + 1) * LANES, :] = hit.T.astype(jnp.bfloat16)
    for p in range(PIECES):
        pltpu.make_async_copy(rbuf.at[p], rbuf.at[p], b_recv.at[p]).wait()
        sums = jnp.dot(assign[...], rbuf[p].reshape(PLANE * 16, PW), preferred_element_type=jnp.float32)
        psum[p] = sums[:128]
        zsend[p] = sums[128:].astype(jnp.bfloat16)
        remote(zsend.at[p], zrecv.at[p], z_send.at[p], z_recv.at[p], z_peer).start()

    def magnitude(p):
        pltpu.make_async_copy(zrecv.at[p], zrecv.at[p], z_recv.at[p]).wait()
        summed = psum[p] + zrecv[p].astype(jnp.float32)
        psum[p] = summed
        re, im = summed[:, :PB], summed[:, PB:]
        mag = jnp.sqrt(re * re + im * im)
        high = mag.astype(jnp.bfloat16)
        mag_hi[p] = high
        mag_lo[p] = (mag - high.astype(jnp.float32)).astype(jnp.bfloat16)

    band_k = lax.broadcasted_iota(jnp.int32, (PW, PB), 0) - LANES
    band_n = lax.broadcasted_iota(jnp.int32, (PW, PB), 1)
    band = jnp.where(jnp.abs(band_k - band_n) <= SMOOTH, 1.0, 0.0).astype(jnp.bfloat16)

    def whiten(p):
        last, following = (p - 1) % PIECES, (p + 1) % PIECES
        level = jnp.zeros((128, PB), jnp.float32)
        for mag in (mag_hi, mag_lo):
            around = jnp.concatenate([mag[last, :, PB - LANES :], mag[p], mag[following, :, :LANES]], axis=1)
            level += jnp.dot(around, band, preferred_element_type=jnp.float32)
        inverse = 1.0 / (level * (1.0 / (2 * SMOOTH + 1)) + EPSILON)
        gath[p, win] = (psum[p] * jnp.concatenate([inverse, inverse], axis=1)).astype(jnp.bfloat16)

    def hand_on(p, source, way):
        item = gath.at[p, source]
        return remote(item, item, g_send.at[p, source, way], g_recv.at[p, source], (sta, win + 1 - 2 * way))

    def serve(p, source):
        for i in range(2):
            w2 = jnp.where(win == 0, 2 + i, i)
            octet = gath.at[p, source, pl.ds(pl.multiple_of(w2 * 32, 32), 32)]
            remote(octet, part.at[p, 1, source], c_send.at[p], c_recv.at[p], ((sta + 2) % STA, w2)).start()

    def begin(p):
        @pl.when(win < WIN - 1)
        def _():
            hand_on(p, win, 0).start()

        @pl.when(win > 0)
        def _():
            hand_on(p, win, 1).start()

        @pl.when((win == 0) | (win == WIN - 1))
        def _():
            serve(p, win)

    def relay(p, d):
        for way in range(2):
            source = win - d if way == 0 else win + d

            @pl.when((source >= 0) & (source < WIN))
            def _(source=source, way=way):
                item = gath.at[p, source]
                pltpu.make_async_copy(item, item, g_recv.at[p, source]).wait()
                last = win == (WIN - 1 if way == 0 else 0)

                @pl.when(jnp.logical_not(last))
                def _():
                    hand_on(p, source, way).start()

                @pl.when(last)
                def _():
                    serve(p, source)

    def swap(p):
        @pl.when(core == 0)
        def _():
            octet = gath.at[p, :, pl.ds(pl.multiple_of(win * 32, 32), 32)]
            remote(octet, part.at[p, 0], x_send.at[p], x_recv.at[p], other_core).start()

        @pl.when(core == 1)
        def _():
            pltpu.make_async_copy(part.at[p, 1], part.at[p, 1], c_recv.at[p]).wait()
            remote(part.at[p, 1], part.at[p, 0], x_send.at[p], x_recv.at[p], other_core).start()

    def finish(p, first):
        @pl.when(core == 0)
        def _():
            pltpu.make_async_copy(part.at[p, 1], part.at[p, 1], c_recv.at[p]).wait()

        pltpu.make_async_copy(part.at[p, 0], part.at[p, 0], x_recv.at[p]).wait()
        part32[...] = part[p].astype(jnp.float32)

        @pl.loop(0, PB // LANES)
        def _(t):
            re = pl.ds(pl.multiple_of(t * LANES, LANES), LANES)
            im = pl.ds(pl.multiple_of(PB + t * LANES, LANES), LANES)
            for g in range(4):
                r = g // 2
                sums = [[[jnp.zeros((8, LANES), jnp.float32) for _ in range(2)] for _ in range(4)] for _ in range(4)]
                for w2 in range(WIN):
                    for pair in range(2):
                        own = []
                        for octet in range(4):
                            at = pl.ds(octet * 32 + pair * 16, 16)
                            own.append(
                                (gath[p, w2, at, re].astype(jnp.float32), gath[p, w2, at, im].astype(jnp.float32))
                            )
                        for e in range(2):
                            for jj in range(4):
                                row = (pair * 2 + e) * 8 + (g % 2) * 4 + jj
                                pr = jnp.broadcast_to(part32[r, w2, row : row + 1, re], (8, LANES))
                                pi = jnp.broadcast_to(part32[r, w2, row : row + 1, im], (8, LANES))
                                for octet in range(4):
                                    a = own[octet][0][e * 8 : e * 8 + 8]
                                    c = own[octet][1][e * 8 : e * 8 + 8]
                                    both = sums[jj][octet]
                                    both[0] = both[0] + pr * a + pi * c
                                    both[1] = both[1] + pr * c - pi * a
                for jj in range(4):
                    at = pl.ds((r * 8 + (g % 2) * 4 + jj) * 32, 32)
                    for half, lanes in enumerate((re, im)):
                        tile = jnp.concatenate([sums[jj][octet][half] for octet in range(4)], axis=0)
                        stack[at, lanes] = tile.astype(jnp.bfloat16)

        @pl.loop(0, LAGS // 512)
        def _(n):
            lanes = pl.ds(pl.multiple_of(n * 512, 512), 512)
            more = jnp.dot(stack[...], table[p, :, lanes], preferred_element_type=jnp.float32)
            if first:
                acc[:, lanes] = more
            else:
                acc[:, lanes] += more

    order = (1, 2, 3, 0)
    for p in range(3):
        magnitude(p)
    for t in range(PIECES + 4):
        if t < PIECES:
            if t == 1:
                magnitude(3)
            whiten(order[t])
            begin(order[t])
        for d in range(1, WIN):
            if 0 <= t - d < PIECES:
                relay(order[t - d], d)
        if t >= 4:
            finish(order[t - 4], t == 4)
        if 0 <= t - 3 < PIECES:
            swap(order[t - 3])
    out[...] = acc[...].astype(jnp.bfloat16).reshape(out.shape)

    def gone(like, semaphore):
        pltpu.make_async_copy(like, like, semaphore).wait()

    gone(tag_s.at[pl.ds(0, 3)], t_send.at[0])
    gone(table.at[0, pl.ds(0, 112), pl.ds(0, 512)], t_send.at[1])
    for p in range(PIECES):
        gone(sbuf.at[p, pl.ds(0, 3)], a_send.at[p])
        gone(table.at[p, pl.ds(0, 112)], b_send.at[p])
        gone(zsend.at[p], z_send.at[p])
        gone(part.at[p, 0], x_send.at[p])

        @pl.when((win == 0) | (win == WIN - 1))
        def _():
            gone(part.at[p], c_send.at[p])

        for d in range(WIN):
            for way in range(2):
                source = win - d if way == 0 else win + d
                more = (source >= 0) & (source < WIN) & (win != (WIN - 1 if way == 0 else 0))

                @pl.when(more)
                def _(source=source, way=way):
                    gone(gath.at[p, source], g_send.at[p, source, way])


def angles(multiples):
    turns = np.outer(multiples, np.arange(LAGS) - LAGS // 2) % (4 * BINS)
    return turns * (2.0 * math.pi / (4 * BINS))


def shards(records, record_block, record_station, quality):
    hours, count, wide = records.shape
    scaling = 1.0 / math.sqrt(2.0 * BINS * hours * WIN)
    coarse, fine = angles(np.arange(BINS // 32) * 32 + 1), angles(np.arange(32))
    cos_u, sin_u = jnp.asarray(np.cos(coarse) * scaling, jnp.float32), jnp.asarray(np.sin(coarse) * scaling, jnp.float32)
    cos_v, sin_v = jnp.asarray(np.cos(fine), jnp.float32), jnp.asarray(np.sin(fine), jnp.float32)
    vmem = pl.BlockSpec(memory_space=pltpu.VMEM)
    dma = pltpu.SemaphoreType.DMA
    bf16, f32 = jnp.bfloat16, jnp.float32
    return pl.pallas_call(
        kernel,
        out_shape=jax.ShapeDtypeStruct((ROUNDS, 8, 32, LAGS), bf16),
        in_specs=[vmem] * 8,
        out_specs=vmem,
        scratch_shapes=[
            pltpu.VMEM((PIECES, 4, 4, 2, 16, PW), bf16),
            pltpu.VMEM((PIECES, 4, 4, 2, 16, PW), bf16),
            pltpu.VMEM((PIECES, 4, 4, 2, 16, PW), bf16),
            pltpu.VMEM((4, 4, 2, 16, LANES), bf16),
            pltpu.VMEM((4, 4, 2, 16, LANES), bf16),
            pltpu.VMEM((4, 4, 2, 16, LANES), bf16),
            pltpu.VMEM((256, PLANE * 16), bf16),
            pltpu.VMEM((PIECES, 128, PW), f32),
            pltpu.VMEM((PIECES, 128, PW), bf16),
            pltpu.VMEM((PIECES, 128, PW), bf16),
            pltpu.VMEM((PIECES, 128, PB), bf16),
            pltpu.VMEM((PIECES, 128, PB), bf16),
            pltpu.VMEM((PIECES, WIN, 128, PW), bf16),
            pltpu.VMEM((PIECES, ROUNDS, WIN, 32, PW), bf16),
            pltpu.VMEM((ROUNDS, WIN, 32, PW), f32),
            pltpu.VMEM((PIECES, PW, LAGS), bf16),
            pltpu.VMEM((512, PW), bf16),
            pltpu.VMEM((512, LAGS), f32),
            dma((PIECES,)), dma((PIECES,)), dma((PIECES,)), dma((PIECES,)), dma((2,)), dma((2,)),
            dma((PIECES,)), dma((PIECES,)), dma((PIECES, WIN, 2)), dma((PIECES, WIN)),
            dma((PIECES,)), dma((PIECES,)), dma((PIECES,)), dma((PIECES,)),
        ],
        compiler_params=pltpu.CompilerParams(
            collective_id=0, has_side_effects=True, vmem_limit_bytes=56 * 2**20
        ),
        name="correlate",
    )(record_block.reshape(hours, 1, count), record_station, quality, records.reshape(hours * count, wide), cos_u, sin_u, cos_v, sin_v)


def solution(mesh):
    in_specs = (P("win", "sta", None), P("win", "sta", None), P("win", "sta"), P("win", "sta"))
    out_specs = P(None, "win", "sta", None)
    return jax.shard_map(shards, mesh=mesh, in_specs=in_specs, out_specs=out_specs, check_vma=False)
```

```python
import math

import jax
import jax.numpy as jnp
import numpy as np
from jax import lax
from jax.experimental import pallas as pl
from jax.experimental.pallas import tpu as pltpu
from jax.sharding import PartitionSpec as P

MESH = pl.DeviceIdType.MESH
BINS = 1024
LAGS = 2048
SMOOTH = 32
ROUNDS = 2
EPSILON = 1e-05
HOURS_DEV = 4
RECS_DEV = 64
WIN = 4
STA = 64
PLANE = 32
PIECES = 4
PB = BINS // PIECES
PW = 2 * PB
LANES = 128

OFFSETS = [(0, 0, 1)] + [
    (dy, dx, dc)
    for dy, dx in (
        (0, 1), (1, 0), (0, 3), (3, 0), (2, 2), (1, 1), (3, 3), (1, 3), (3, 1), (0, 2), (2, 0), (1, 2), (2, 1), (3, 2), (2, 3)
    )
    for dc in range(2)
]


def remote(src, dst, send, recv, device):
    return pltpu.make_async_remote_copy(
        src_ref=src, dst_ref=dst, send_sem=send, recv_sem=recv, device_id=device, device_id_type=MESH
    )


def kernel(
    blocks, stations, quality, rec, cos_u, sin_u, cos_v, sin_v, out,
    sbuf, rbuf, tag_s, tag_r, assign, psum, zsend, zrecv, mag_hi, mag_lo, gath, part, part32, table, stack, acc,
    b_send, b_recv, t_send, t_recv, z_send, z_recv, g_send, g_recv, c_send, c_recv, x_send, x_recv,
):
    sta, win = lax.axis_index("sta"), lax.axis_index("win")
    y, x, zh, core = sta // 16, (sta // 4) % 4, (sta // 2) % 2, sta % 2

    slot = (sta // 4) * 2 + core

    def plane_peer(offset):
        y2, x2, c2 = (y + offset[0]) % 4, (x + offset[1]) % 4, (core + offset[2]) % 2
        return (((y2 * 4 + x2) * 2 + zh) * 2 + c2, win), (y2 * 4 + x2) * 2 + c2

    z_peer = (sta + 2 - 4 * zh, win)
    other_core = (sta + 1 - 2 * core, win)

    barrier = pltpu.get_barrier_semaphore()
    greeted = [plane_peer(o)[0] for o in OFFSETS] + [z_peer] + [(sta, (win + d) % WIN) for d in range(1, WIN)]
    greeted += [((sta + d) % STA, w2) for d in (2, STA - 2) for w2 in range(WIN)]
    for device in greeted:
        pl.semaphore_signal(barrier, inc=1, device_id=device, device_id_type=MESH)

    count = HOURS_DEV * RECS_DEV
    hour_row = lax.broadcasted_iota(jnp.int32, (1, count), 1) // RECS_DEV
    block = jnp.concatenate([blocks[h] for h in range(HOURS_DEV)], axis=1)
    station = jnp.concatenate([stations[h : h + 1, :] for h in range(HOURS_DEV)], axis=1)
    passed = jnp.concatenate([quality[h : h + 1, :] for h in range(HOURS_DEV)], axis=1)
    key = (block + hour_row * STA).astype(jnp.float32)
    from_row = lax.broadcasted_iota(jnp.int32, (count, count), 0)
    to_row = lax.broadcasted_iota(jnp.int32, (count, count), 1)
    key_col = jnp.sum(jnp.where(from_row == to_row, key, 0.0), axis=1, keepdims=True)
    earlier = (from_row < to_row) & (key_col == key)
    rank = jnp.sum(jnp.where(earlier, 1.0, 0.0), axis=0, keepdims=True).astype(jnp.int32)
    target = ((block // 4) * 2 + block % 2) * 16 + hour_row * 4 + ((block // 2) % 2) * 2 + rank
    target = jnp.where(passed > 0, target, -1)
    chosen = lax.broadcasted_iota(jnp.int32, (PLANE * 16, count), 0) == target
    tags = jnp.sum(jnp.where(chosen, (station + 1).astype(jnp.float32), 0.0), axis=1, keepdims=True)
    tag_s[...] = jnp.broadcast_to(tags, (PLANE * 16, LANES)).astype(jnp.bfloat16).reshape(tag_s.shape)
    placing = jnp.where(chosen, 1.0, 0.0).astype(jnp.bfloat16)

    pl.semaphore_wait(barrier, len(greeted))

    def spread(source, arrived, send, recv):
        for offset in OFFSETS:
            device, place = plane_peer(offset)
            remote(source.at[place], arrived.at[slot], send, recv, device).start()
        pltpu.make_async_copy(source.at[slot], arrived.at[slot], recv).start()

    spread(tag_s, tag_r, t_send, t_recv)
    for p in range(PIECES):
        for half in range(2):
            lanes = pl.ds(half * BINS + p * PB, PB)
            packed = jnp.dot(placing, rec[:, lanes], preferred_element_type=jnp.float32)
            sbuf[p, :, :, half * PB : (half + 1) * PB] = packed.astype(jnp.bfloat16).reshape(PLANE, 16, PB)
        spread(sbuf.at[p], rbuf.at[p], b_send.at[p], b_recv.at[p])

    def weigh(p):
        @pl.loop(0, PB // 32)
        def _(i):
            u = p * (PB // 32) + i
            row = pl.multiple_of(i * 32, 32)
            for n in range(LAGS // 512):
                lanes = pl.ds(n * 512, 512)
                cu, su = cos_u[pl.ds(u, 1), lanes], sin_u[pl.ds(u, 1), lanes]
                cv, sv = cos_v[:, lanes], sin_v[:, lanes]
                table[p, pl.ds(row, 32), lanes] = (cu * cv - su * sv).astype(jnp.bfloat16)
                table[p, pl.ds(PB + row, 32), lanes] = (-(su * cv) - cu * sv).astype(jnp.bfloat16)

    for p in range(PIECES):
        weigh(p)

    pltpu.make_async_copy(tag_r, tag_r, t_recv).wait()
    label = tag_r[...].astype(jnp.float32).astype(jnp.int32).reshape(PLANE * 16, LANES) - 1
    row_id = lax.broadcasted_iota(jnp.int32, (PLANE * 16, LANES), 0)
    member = ((row_id // 2 + zh) % 2) * 128 + (label // 8) * 32 + ((row_id // 4) % 4) * 8 + label % 8
    member = jnp.where(label >= 0, member, -1)
    lane_id = lax.broadcasted_iota(jnp.int32, (PLANE * 16, LANES), 1)
    for half in range(2):
        hit = jnp.where(member == lane_id + half * LANES, 1.0, 0.0)
        assign[half * LANES : (half + 1) * LANES, :] = hit.T.astype(jnp.bfloat16)
    for p in range(PIECES):
        pltpu.make_async_copy(rbuf.at[p], rbuf.at[p], b_recv.at[p]).wait()
        sums = jnp.dot(assign[...], rbuf[p].reshape(PLANE * 16, PW), preferred_element_type=jnp.float32)
        psum[p] = sums[:128]
        zsend[p] = sums[128:].astype(jnp.bfloat16)
        remote(zsend.at[p], zrecv.at[p], z_send.at[p], z_recv.at[p], z_peer).start()

    def magnitude(p):
        pltpu.make_async_copy(zrecv.at[p], zrecv.at[p], z_recv.at[p]).wait()
        summed = psum[p] + zrecv[p].astype(jnp.float32)
        psum[p] = summed
        re, im = summed[:, :PB], summed[:, PB:]
        mag = jnp.sqrt(re * re + im * im)
        high = mag.astype(jnp.bfloat16)
        mag_hi[p] = high
        mag_lo[p] = (mag - high.astype(jnp.float32)).astype(jnp.bfloat16)

    band_k = lax.broadcasted_iota(jnp.int32, (PW, PB), 0) - LANES
    band_n = lax.broadcasted_iota(jnp.int32, (PW, PB), 1)
    band = jnp.where(jnp.abs(band_k - band_n) <= SMOOTH, 1.0, 0.0).astype(jnp.bfloat16)

    def whiten(p):
        last, following = (p - 1) % PIECES, (p + 1) % PIECES
        level = jnp.zeros((128, PB), jnp.float32)
        for mag in (mag_hi, mag_lo):
            around = jnp.concatenate([mag[last, :, PB - LANES :], mag[p], mag[following, :, :LANES]], axis=1)
            level += jnp.dot(around, band, preferred_element_type=jnp.float32)
        inverse = 1.0 / (level * (1.0 / (2 * SMOOTH + 1)) + EPSILON)
        gath[p, win] = (psum[p] * jnp.concatenate([inverse, inverse], axis=1)).astype(jnp.bfloat16)

    def hand_on(p, source, way):
        item = gath.at[p, source]
        return remote(item, item, g_send.at[p, source, way], g_recv.at[p, source], (sta, win + 1 - 2 * way))

    def serve(p, source):
        for i in range(2):
            w2 = jnp.where(win == 0, 2 + i, i)
            octet = gath.at[p, source, pl.ds(pl.multiple_of(w2 * 32, 32), 32)]
            remote(octet, part.at[p, 1, source], c_send.at[p], c_recv.at[p], ((sta + 2) % STA, w2)).start()

    def begin(p):
        @pl.when(win < WIN - 1)
        def _():
            hand_on(p, win, 0).start()

        @pl.when(win > 0)
        def _():
            hand_on(p, win, 1).start()

        @pl.when((win == 0) | (win == WIN - 1))
        def _():
            serve(p, win)

    def relay(p, d):
        for way in range(2):
            source = win - d if way == 0 else win + d

            @pl.when((source >= 0) & (source < WIN))
            def _(source=source, way=way):
                item = gath.at[p, source]
                pltpu.make_async_copy(item, item, g_recv.at[p, source]).wait()
                last = win == (WIN - 1 if way == 0 else 0)

                @pl.when(jnp.logical_not(last))
                def _():
                    hand_on(p, source, way).start()

                @pl.when(last)
                def _():
                    serve(p, source)

    def swap(p):
        @pl.when(core == 0)
        def _():
            octet = gath.at[p, :, pl.ds(pl.multiple_of(win * 32, 32), 32)]
            remote(octet, part.at[p, 0], x_send.at[p], x_recv.at[p], other_core).start()

        @pl.when(core == 1)
        def _():
            pltpu.make_async_copy(part.at[p, 1], part.at[p, 1], c_recv.at[p]).wait()
            remote(part.at[p, 1], part.at[p, 0], x_send.at[p], x_recv.at[p], other_core).start()

    def finish(p, first):
        @pl.when(core == 0)
        def _():
            pltpu.make_async_copy(part.at[p, 1], part.at[p, 1], c_recv.at[p]).wait()

        pltpu.make_async_copy(part.at[p, 0], part.at[p, 0], x_recv.at[p]).wait()
        part32[...] = part[p].astype(jnp.float32)

        @pl.loop(0, PB // LANES)
        def _(t):
            re = pl.ds(pl.multiple_of(t * LANES, LANES), LANES)
            im = pl.ds(pl.multiple_of(PB + t * LANES, LANES), LANES)
            for g in range(4):
                r = g // 2
                sums = [[[jnp.zeros((8, LANES), jnp.float32) for _ in range(2)] for _ in range(4)] for _ in range(4)]
                for w2 in range(WIN):
                    for pair in range(2):
                        own = []
                        for octet in range(4):
                            at = pl.ds(octet * 32 + pair * 16, 16)
                            own.append(
                                (gath[p, w2, at, re].astype(jnp.float32), gath[p, w2, at, im].astype(jnp.float32))
                            )
                        for e in range(2):
                            for jj in range(4):
                                row = (pair * 2 + e) * 8 + (g % 2) * 4 + jj
                                pr = jnp.broadcast_to(part32[r, w2, row : row + 1, re], (8, LANES))
                                pi = jnp.broadcast_to(part32[r, w2, row : row + 1, im], (8, LANES))
                                for octet in range(4):
                                    a = own[octet][0][e * 8 : e * 8 + 8]
                                    c = own[octet][1][e * 8 : e * 8 + 8]
                                    both = sums[jj][octet]
                                    both[0] = both[0] + pr * a + pi * c
                                    both[1] = both[1] + pr * c - pi * a
                for jj in range(4):
                    at = pl.ds((r * 8 + (g % 2) * 4 + jj) * 32, 32)
                    for half, lanes in enumerate((re, im)):
                        tile = jnp.concatenate([sums[jj][octet][half] for octet in range(4)], axis=0)
                        stack[at, lanes] = tile.astype(jnp.bfloat16)

        @pl.loop(0, LAGS // 512)
        def _(n):
            lanes = pl.ds(pl.multiple_of(n * 512, 512), 512)
            more = jnp.dot(stack[...], table[p, :, lanes], preferred_element_type=jnp.float32)
            if first:
                acc[:, lanes] = more
            else:
                acc[:, lanes] += more

    order = (1, 2, 3, 0)
    for p in range(3):
        magnitude(p)
    for t in range(PIECES + 4):
        if t < PIECES:
            if t == 1:
                magnitude(3)
            whiten(order[t])
            begin(order[t])
        for d in range(1, WIN):
            if 0 <= t - d < PIECES:
                relay(order[t - d], d)
        if t >= 4:
            finish(order[t - 4], t == 4)
        if 0 <= t - 3 < PIECES:
            swap(order[t - 3])
    out[...] = acc[...].astype(jnp.bfloat16).reshape(out.shape)

    def gone(like, semaphore):
        pltpu.make_async_copy(like, like, semaphore).wait()

    gone(tag_s.at[pl.ds(0, PLANE - 1)], t_send)
    for p in range(PIECES):
        gone(sbuf.at[p, pl.ds(0, PLANE - 1)], b_send.at[p])
        gone(zsend.at[p], z_send.at[p])
        gone(part.at[p, 0], x_send.at[p])

        @pl.when((win == 0) | (win == WIN - 1))
        def _():
            gone(part.at[p], c_send.at[p])

        for d in range(WIN):
            for way in range(2):
                source = win - d if way == 0 else win + d
                more = (source >= 0) & (source < WIN) & (win != (WIN - 1 if way == 0 else 0))

                @pl.when(more)
                def _(source=source, way=way):
                    gone(gath.at[p, source], g_send.at[p, source, way])


def angles(multiples):
    turns = np.outer(multiples, np.arange(LAGS) - LAGS // 2) % (4 * BINS)
    return turns * (2.0 * math.pi / (4 * BINS))


def shards(records, record_block, record_station, quality):
    hours, count, wide = records.shape
    scaling = 1.0 / math.sqrt(2.0 * BINS * hours * WIN)
    coarse, fine = angles(np.arange(BINS // 32) * 32 + 1), angles(np.arange(32))
    cos_u, sin_u = jnp.asarray(np.cos(coarse) * scaling, jnp.float32), jnp.asarray(np.sin(coarse) * scaling, jnp.float32)
    cos_v, sin_v = jnp.asarray(np.cos(fine), jnp.float32), jnp.asarray(np.sin(fine), jnp.float32)
    vmem = pl.BlockSpec(memory_space=pltpu.VMEM)
    dma = pltpu.SemaphoreType.DMA
    bf16, f32 = jnp.bfloat16, jnp.float32
    return pl.pallas_call(
        kernel,
        out_shape=jax.ShapeDtypeStruct((ROUNDS, 8, 32, LAGS), bf16),
        in_specs=[vmem] * 8,
        out_specs=vmem,
        scratch_shapes=[
            pltpu.VMEM((PIECES, PLANE, 16, PW), bf16),
            pltpu.VMEM((PIECES, PLANE, 16, PW), bf16),
            pltpu.VMEM((PLANE, 16, LANES), bf16),
            pltpu.VMEM((PLANE, 16, LANES), bf16),
            pltpu.VMEM((256, PLANE * 16), bf16),
            pltpu.VMEM((PIECES, 128, PW), f32),
            pltpu.VMEM((PIECES, 128, PW), bf16),
            pltpu.VMEM((PIECES, 128, PW), bf16),
            pltpu.VMEM((PIECES, 128, PB), bf16),
            pltpu.VMEM((PIECES, 128, PB), bf16),
            pltpu.VMEM((PIECES, WIN, 128, PW), bf16),
            pltpu.VMEM((PIECES, ROUNDS, WIN, 32, PW), bf16),
            pltpu.VMEM((ROUNDS, WIN, 32, PW), f32),
            pltpu.VMEM((PIECES, PW, LAGS), bf16),
            pltpu.VMEM((512, PW), bf16),
            pltpu.VMEM((512, LAGS), f32),
            dma((PIECES,)), dma((PIECES,)), dma, dma,
            dma((PIECES,)), dma((PIECES,)), dma((PIECES, WIN, 2)), dma((PIECES, WIN)),
            dma((PIECES,)), dma((PIECES,)), dma((PIECES,)), dma((PIECES,)),
        ],
        compiler_params=pltpu.CompilerParams(
            collective_id=0, has_side_effects=True, vmem_limit_bytes=56 * 2**20
        ),
        name="correlate",
    )(record_block.reshape(hours, 1, count), record_station, quality, records.reshape(hours * count, wide), cos_u, sin_u, cos_v, sin_v)


def solution(mesh):
    in_specs = (P("win", "sta", None), P("win", "sta", None), P("win", "sta"), P("win", "sta"))
    out_specs = P(None, "win", "sta", None)
    return jax.shard_map(shards, mesh=mesh, in_specs=in_specs, out_specs=out_specs, check_vma=False)
```

```python
import math

import jax
import jax.numpy as jnp
import numpy as np
from jax import lax
from jax.experimental import pallas as pl
from jax.experimental.pallas import tpu as pltpu
from jax.sharding import PartitionSpec as P

MESH = pl.DeviceIdType.MESH
BINS = 1024
LAGS = 2048
SMOOTH = 32
ROUNDS = 2
EPSILON = 1e-05
HOURS_DEV = 4
RECS_DEV = 64
WIN = 4
STA = 64
PLANE = 32
PIECES = 4
PB = BINS // PIECES
PW = 2 * PB
LANES = 128

OFFSETS = [(0, 0, 1)] + [
    (dy, dx, dc)
    for dy, dx in (
        (0, 1), (1, 0), (0, 3), (3, 0), (2, 2), (1, 1), (3, 3), (1, 3), (3, 1), (0, 2), (2, 0), (1, 2), (2, 1), (3, 2), (2, 3)
    )
    for dc in range(2)
]


def remote(src, dst, send, recv, device):
    return pltpu.make_async_remote_copy(
        src_ref=src, dst_ref=dst, send_sem=send, recv_sem=recv, device_id=device, device_id_type=MESH
    )


def kernel(
    blocks, stations, quality, rec, cos_u, sin_u, cos_v, sin_v, out,
    sbuf, rbuf, tag_s, tag_r, assign, psum, zsend, zrecv, mag_hi, mag_lo, gath, part, part32, table, stack, acc,
    b_send, b_recv, t_send, t_recv, z_send, z_recv, g_send, g_recv, c_send, c_recv, x_send, x_recv,
):
    sta, win = lax.axis_index("sta"), lax.axis_index("win")
    y, x, zh, core = sta // 16, (sta // 4) % 4, (sta // 2) % 2, sta % 2

    slot = (sta // 4) * 2 + core

    def plane_peer(offset):
        y2, x2, c2 = (y + offset[0]) % 4, (x + offset[1]) % 4, (core + offset[2]) % 2
        return (((y2 * 4 + x2) * 2 + zh) * 2 + c2, win), (y2 * 4 + x2) * 2 + c2

    z_peer = (sta + 2 - 4 * zh, win)
    other_core = (sta + 1 - 2 * core, win)

    barrier = pltpu.get_barrier_semaphore()
    greeted = [plane_peer(o)[0] for o in OFFSETS] + [z_peer] + [(sta, (win + d) % WIN) for d in range(1, WIN)]
    greeted += [((sta + d) % STA, w2) for d in (2, STA - 2) for w2 in range(WIN)]
    for device in greeted:
        pl.semaphore_signal(barrier, inc=1, device_id=device, device_id_type=MESH)

    count = HOURS_DEV * RECS_DEV
    hour_row = lax.broadcasted_iota(jnp.int32, (1, count), 1) // RECS_DEV
    block = jnp.concatenate([blocks[h] for h in range(HOURS_DEV)], axis=1)
    station = jnp.concatenate([stations[h : h + 1, :] for h in range(HOURS_DEV)], axis=1)
    passed = jnp.concatenate([quality[h : h + 1, :] for h in range(HOURS_DEV)], axis=1)
    key = (block + hour_row * STA).astype(jnp.float32)
    from_row = lax.broadcasted_iota(jnp.int32, (count, count), 0)
    to_row = lax.broadcasted_iota(jnp.int32, (count, count), 1)
    key_col = jnp.sum(jnp.where(from_row == to_row, key, 0.0), axis=1, keepdims=True)
    earlier = (from_row < to_row) & (key_col == key)
    rank = jnp.sum(jnp.where(earlier, 1.0, 0.0), axis=0, keepdims=True).astype(jnp.int32)
    target = ((block // 4) * 2 + block % 2) * 16 + hour_row * 4 + ((block // 2) % 2) * 2 + rank
    target = jnp.where(passed > 0, target, -1)
    chosen = lax.broadcasted_iota(jnp.int32, (PLANE * 16, count), 0) == target
    tags = jnp.sum(jnp.where(chosen, (station + 1).astype(jnp.float32), 0.0), axis=1, keepdims=True)
    tag_s[...] = jnp.broadcast_to(tags, (PLANE * 16, LANES)).astype(jnp.bfloat16).reshape(tag_s.shape)
    placing = jnp.where(chosen, 1.0, 0.0).astype(jnp.bfloat16)

    pl.semaphore_wait(barrier, len(greeted))

    def spread(source, arrived, send, recv):
        for offset in OFFSETS:
            device, place = plane_peer(offset)
            remote(source.at[place], arrived.at[slot], send, recv, device).start()
        pltpu.make_async_copy(source.at[slot], arrived.at[slot], recv).start()

    spread(tag_s, tag_r, t_send, t_recv)
    for p in range(PIECES):
        for half in range(2):
            lanes = pl.ds(half * BINS + p * PB, PB)
            packed = jnp.dot(placing, rec[:, lanes], preferred_element_type=jnp.float32)
            sbuf[p, :, :, half * PB : (half + 1) * PB] = packed.astype(jnp.bfloat16).reshape(PLANE, 16, PB)
        spread(sbuf.at[p], rbuf.at[p], b_send.at[p], b_recv.at[p])

    def weigh(p):
        @pl.loop(0, PB // 32)
        def _(i):
            u = p * (PB // 32) + i
            row = pl.multiple_of(i * 32, 32)
            for n in range(LAGS // 512):
                lanes = pl.ds(n * 512, 512)
                cu, su = cos_u[pl.ds(u, 1), lanes], sin_u[pl.ds(u, 1), lanes]
                cv, sv = cos_v[:, lanes], sin_v[:, lanes]
                table[p, pl.ds(row, 32), lanes] = (cu * cv - su * sv).astype(jnp.bfloat16)
                table[p, pl.ds(PB + row, 32), lanes] = (-(su * cv) - cu * sv).astype(jnp.bfloat16)

    for p in range(PIECES):
        weigh(p)

    pltpu.make_async_copy(tag_r, tag_r, t_recv).wait()
    label = tag_r[...].astype(jnp.float32).astype(jnp.int32).reshape(PLANE * 16, LANES) - 1
    row_id = lax.broadcasted_iota(jnp.int32, (PLANE * 16, LANES), 0)
    member = ((row_id // 2 + zh) % 2) * 128 + (label // 8) * 32 + ((row_id // 4) % 4) * 8 + label % 8
    member = jnp.where(label >= 0, member, -1)
    lane_id = lax.broadcasted_iota(jnp.int32, (PLANE * 16, LANES), 1)
    for half in range(2):
        hit = jnp.where(member == lane_id + half * LANES, 1.0, 0.0)
        assign[half * LANES : (half + 1) * LANES, :] = hit.T.astype(jnp.bfloat16)
    for p in range(PIECES):
        pltpu.make_async_copy(rbuf.at[p], rbuf.at[p], b_recv.at[p]).wait()
        sums = jnp.dot(assign[...], rbuf[p].reshape(PLANE * 16, PW), preferred_element_type=jnp.float32)
        psum[p] = sums[:128]
        zsend[p] = sums[128:].astype(jnp.bfloat16)
        remote(zsend.at[p], zrecv.at[p], z_send.at[p], z_recv.at[p], z_peer).start()

    def magnitude(p):
        pltpu.make_async_copy(zrecv.at[p], zrecv.at[p], z_recv.at[p]).wait()
        summed = psum[p] + zrecv[p].astype(jnp.float32)
        psum[p] = summed
        re, im = summed[:, :PB], summed[:, PB:]
        mag = jnp.sqrt(re * re + im * im)
        high = mag.astype(jnp.bfloat16)
        mag_hi[p] = high
        mag_lo[p] = (mag - high.astype(jnp.float32)).astype(jnp.bfloat16)

    band_k = lax.broadcasted_iota(jnp.int32, (PW, PB), 0) - LANES
    band_n = lax.broadcasted_iota(jnp.int32, (PW, PB), 1)
    band = jnp.where(jnp.abs(band_k - band_n) <= SMOOTH, 1.0, 0.0).astype(jnp.bfloat16)

    def whiten(p):
        last, following = (p - 1) % PIECES, (p + 1) % PIECES
        level = jnp.zeros((128, PB), jnp.float32)
        for mag in (mag_hi, mag_lo):
            around = jnp.concatenate([mag[last, :, PB - LANES :], mag[p], mag[following, :, :LANES]], axis=1)
            level += jnp.dot(around, band, preferred_element_type=jnp.float32)
        inverse = 1.0 / (level * (1.0 / (2 * SMOOTH + 1)) + EPSILON)
        gath[p, win] = (psum[p] * jnp.concatenate([inverse, inverse], axis=1)).astype(jnp.bfloat16)

    def hand_on(p, source, way):
        item = gath.at[p, source]
        return remote(item, item, g_send.at[p, source, way], g_recv.at[p, source], (sta, win + 1 - 2 * way))

    def serve(p, source):
        for i in range(2):
            w2 = jnp.where(win == 0, 2 + i, i)
            octet = gath.at[p, source, pl.ds(pl.multiple_of(w2 * 32, 32), 32)]
            remote(octet, part.at[p, 1, source], c_send.at[p], c_recv.at[p], ((sta + 2) % STA, w2)).start()

    def begin(p):
        @pl.when(win < WIN - 1)
        def _():
            hand_on(p, win, 0).start()

        @pl.when(win > 0)
        def _():
            hand_on(p, win, 1).start()

        @pl.when((win == 0) | (win == WIN - 1))
        def _():
            serve(p, win)

    def relay(p, d):
        for way in range(2):
            source = win - d if way == 0 else win + d

            @pl.when((source >= 0) & (source < WIN))
            def _(source=source, way=way):
                item = gath.at[p, source]
                pltpu.make_async_copy(item, item, g_recv.at[p, source]).wait()
                last = win == (WIN - 1 if way == 0 else 0)

                @pl.when(jnp.logical_not(last))
                def _():
                    hand_on(p, source, way).start()

                @pl.when(last)
                def _():
                    serve(p, source)

    def swap_own(p):
        @pl.when(core == 0)
        def _():
            octet = gath.at[p, :, pl.ds(pl.multiple_of(win * 32, 32), 32)]
            remote(octet, part.at[p, 0], x_send.at[p], x_recv.at[p], other_core).start()

    def swap(p):
        @pl.when(core == 1)
        def _():
            pltpu.make_async_copy(part.at[p, 1], part.at[p, 1], c_recv.at[p]).wait()
            remote(part.at[p, 1], part.at[p, 0], x_send.at[p], x_recv.at[p], other_core).start()

    def finish(p, first):
        @pl.when(core == 0)
        def _():
            pltpu.make_async_copy(part.at[p, 1], part.at[p, 1], c_recv.at[p]).wait()

        pltpu.make_async_copy(part.at[p, 0], part.at[p, 0], x_recv.at[p]).wait()
        part32[...] = part[p].astype(jnp.float32)

        @pl.loop(0, PB // LANES)
        def _(t):
            re = pl.ds(pl.multiple_of(t * LANES, LANES), LANES)
            im = pl.ds(pl.multiple_of(PB + t * LANES, LANES), LANES)
            for g in range(4):
                r = g // 2
                sums = [[[jnp.zeros((8, LANES), jnp.float32) for _ in range(3)] for _ in range(4)] for _ in range(4)]
                for w2 in range(WIN):
                    for pair in range(2):
                        own = []
                        for octet in range(4):
                            at = pl.ds(octet * 32 + pair * 16, 16)
                            a, c = gath[p, w2, at, re].astype(jnp.float32), gath[p, w2, at, im].astype(jnp.float32)
                            own.append((a, c, a + c))
                        for e in range(2):
                            for jj in range(4):
                                row = (pair * 2 + e) * 8 + (g % 2) * 4 + jj
                                pr = jnp.broadcast_to(part32[r, w2, row : row + 1, re], (8, LANES))
                                pi = jnp.broadcast_to(part32[r, w2, row : row + 1, im], (8, LANES))
                                pd = pr - pi
                                for octet in range(4):
                                    a, c, ac = (v[e * 8 : e * 8 + 8] for v in own[octet])
                                    three = sums[jj][octet]
                                    three[0] = three[0] + pr * a
                                    three[1] = three[1] + pi * c
                                    three[2] = three[2] + pd * ac
                for jj in range(4):
                    at = pl.ds((r * 8 + (g % 2) * 4 + jj) * 32, 32)
                    for half, lanes in enumerate((re, im)):
                        tile = jnp.concatenate(
                            [s[2] - s[0] + s[1] if half else s[0] + s[1] for s in sums[jj]], axis=0
                        )
                        stack[at, lanes] = tile.astype(jnp.bfloat16)

        @pl.loop(0, LAGS // 512)
        def _(n):
            lanes = pl.ds(pl.multiple_of(n * 512, 512), 512)
            more = jnp.dot(stack[...], table[p, :, lanes], preferred_element_type=jnp.float32)
            if first:
                acc[:, lanes] = more
            else:
                acc[:, lanes] += more

    order = (1, 2, 3, 0)
    for p in range(3):
        magnitude(p)
    for t in range(PIECES + 4):
        if t < PIECES:
            if t == 1:
                magnitude(3)
            whiten(order[t])
            begin(order[t])
        for d in (3, 2, 1):
            if 0 <= t - d < PIECES:
                relay(order[t - d], d)
                if d == 3:
                    swap_own(order[t - d])
        if t >= 4:
            finish(order[t - 4], t == 4)
        if 0 <= t - 3 < PIECES:
            swap(order[t - 3])
    out[...] = acc[...].astype(jnp.bfloat16).reshape(out.shape)

    def gone(like, semaphore):
        pltpu.make_async_copy(like, like, semaphore).wait()

    gone(tag_s.at[pl.ds(0, PLANE - 1)], t_send)
    for p in range(PIECES):
        gone(sbuf.at[p, pl.ds(0, PLANE - 1)], b_send.at[p])
        gone(zsend.at[p], z_send.at[p])
        gone(part.at[p, 0], x_send.at[p])

        @pl.when((win == 0) | (win == WIN - 1))
        def _():
            gone(part.at[p], c_send.at[p])

        for d in range(WIN):
            for way in range(2):
                source = win - d if way == 0 else win + d
                more = (source >= 0) & (source < WIN) & (win != (WIN - 1 if way == 0 else 0))

                @pl.when(more)
                def _(source=source, way=way):
                    gone(gath.at[p, source], g_send.at[p, source, way])


def hand_over(src, dst, held, came, left):
    places = [(r, pl.ds(j, 2)) for r in range(ROUNDS) for j in range(0, 8, 2)]
    into = [pltpu.make_async_copy(src.at[at], held.at[at], came.at[i]) for i, at in enumerate(places)]
    onto = [pltpu.make_async_copy(held.at[at], dst.at[at], left.at[i]) for i, at in enumerate(places)]
    for copy in into:
        copy.start()
    for before, after in zip(into, onto):
        before.wait()
        after.start()
    for copy in onto:
        copy.wait()


def angles(multiples):
    turns = np.outer(multiples, np.arange(LAGS) - LAGS // 2) % (4 * BINS)
    return turns * (2.0 * math.pi / (4 * BINS))


def shards(records, record_block, record_station, quality):
    hours, count, wide = records.shape
    scaling = 1.0 / math.sqrt(2.0 * BINS * hours * WIN)
    coarse, fine = angles(np.arange(BINS // 32) * 32 + 1), angles(np.arange(32))
    cos_u, sin_u = jnp.asarray(np.cos(coarse) * scaling, jnp.float32), jnp.asarray(np.sin(coarse) * scaling, jnp.float32)
    cos_v, sin_v = jnp.asarray(np.cos(fine), jnp.float32), jnp.asarray(np.sin(fine), jnp.float32)
    vmem = pl.BlockSpec(memory_space=pltpu.VMEM)
    dma = pltpu.SemaphoreType.DMA
    bf16, f32 = jnp.bfloat16, jnp.float32
    result = pl.pallas_call(
        kernel,
        out_shape=jax.ShapeDtypeStruct((ROUNDS, 8, 32, LAGS), bf16),
        in_specs=[vmem] * 8,
        out_specs=vmem,
        scratch_shapes=[
            pltpu.VMEM((PIECES, PLANE, 16, PW), bf16),
            pltpu.VMEM((PIECES, PLANE, 16, PW), bf16),
            pltpu.VMEM((PLANE, 16, LANES), bf16),
            pltpu.VMEM((PLANE, 16, LANES), bf16),
            pltpu.VMEM((256, PLANE * 16), bf16),
            pltpu.VMEM((PIECES, 128, PW), f32),
            pltpu.VMEM((PIECES, 128, PW), bf16),
            pltpu.VMEM((PIECES, 128, PW), bf16),
            pltpu.VMEM((PIECES, 128, PB), bf16),
            pltpu.VMEM((PIECES, 128, PB), bf16),
            pltpu.VMEM((PIECES, WIN, 128, PW), bf16),
            pltpu.VMEM((PIECES, ROUNDS, WIN, 32, PW), bf16),
            pltpu.VMEM((ROUNDS, WIN, 32, PW), f32),
            pltpu.VMEM((PIECES, PW, LAGS), bf16),
            pltpu.VMEM((512, PW), bf16),
            pltpu.VMEM((512, LAGS), f32),
            dma((PIECES,)), dma((PIECES,)), dma, dma,
            dma((PIECES,)), dma((PIECES,)), dma((PIECES, WIN, 2)), dma((PIECES, WIN)),
            dma((PIECES,)), dma((PIECES,)), dma((PIECES,)), dma((PIECES,)),
        ],
        compiler_params=pltpu.CompilerParams(
            collective_id=0, has_side_effects=True, vmem_limit_bytes=56 * 2**20
        ),
        name="correlate",
    )(record_block.reshape(hours, 1, count), record_station, quality, records.reshape(hours * count, wide), cos_u, sin_u, cos_v, sin_v)
    anywhere = pl.BlockSpec(memory_space=pl.ANY)
    return pl.pallas_call(
        hand_over,
        out_shape=jax.ShapeDtypeStruct(result.shape, result.dtype),
        in_specs=[anywhere],
        out_specs=anywhere,
        scratch_shapes=[pltpu.VMEM(result.shape, bf16), dma((8,)), dma((8,))],
        name="hand_over",
    )(result)


def solution(mesh):
    in_specs = (P("win", "sta", None), P("win", "sta", None), P("win", "sta"), P("win", "sta"))
    out_specs = P(None, "win", "sta", None)
    return jax.shard_map(shards, mesh=mesh, in_specs=in_specs, out_specs=out_specs, check_vma=False)
```

```python
import math

import jax
import jax.numpy as jnp
import numpy as np
from jax import lax
from jax.experimental import pallas as pl
from jax.experimental.pallas import tpu as pltpu
from jax.sharding import PartitionSpec as P

MESH = pl.DeviceIdType.MESH
BINS = 1024
LAGS = 2048
SMOOTH = 32
ROUNDS = 2
EPSILON = 1e-05
HOURS_DEV = 4
RECS_DEV = 64
WIN = 4
STA = 64
PLANE = 32
PIECES = 4
PB = BINS // PIECES
PW = 2 * PB
LANES = 128

OFFSETS = [(0, 0, 1)] + [
    (dy, dx, dc)
    for dy, dx in (
        (0, 1), (1, 0), (0, 3), (3, 0), (2, 2), (1, 1), (3, 3), (1, 3), (3, 1), (0, 2), (2, 0), (1, 2), (2, 1), (3, 2), (2, 3)
    )
    for dc in range(2)
]


def remote(src, dst, send, recv, device):
    return pltpu.make_async_remote_copy(
        src_ref=src, dst_ref=dst, send_sem=send, recv_sem=recv, device_id=device, device_id_type=MESH
    )


def kernel(
    blocks, stations, quality, rec, cos_u, sin_u, cos_v, sin_v, out,
    sbuf, rbuf, tag_s, tag_r, assign, psum, zsend, zrecv, mag_hi, mag_lo, gath, part, part32, table, stack, acc,
    b_send, b_recv, t_send, t_recv, z_send, z_recv, g_send, g_recv, c_send, c_recv, x_send, x_recv,
):
    sta, win = lax.axis_index("sta"), lax.axis_index("win")
    y, x, zh, core = sta // 16, (sta // 4) % 4, (sta // 2) % 2, sta % 2

    slot = (sta // 4) * 2 + core

    def plane_peer(offset):
        y2, x2, c2 = (y + offset[0]) % 4, (x + offset[1]) % 4, (core + offset[2]) % 2
        return (((y2 * 4 + x2) * 2 + zh) * 2 + c2, win), (y2 * 4 + x2) * 2 + c2

    z_peer = (sta + 2 - 4 * zh, win)
    other_core = (sta + 1 - 2 * core, win)

    barrier = pltpu.get_barrier_semaphore()
    greeted = [plane_peer(o)[0] for o in OFFSETS] + [z_peer] + [(sta, (win + d) % WIN) for d in range(1, WIN)]
    greeted += [((sta + d) % STA, w2) for d in (2, STA - 2) for w2 in range(WIN)]
    for device in greeted:
        pl.semaphore_signal(barrier, inc=1, device_id=device, device_id_type=MESH)

    count = HOURS_DEV * RECS_DEV
    hour_row = lax.broadcasted_iota(jnp.int32, (1, count), 1) // RECS_DEV
    block = jnp.concatenate([blocks[h] for h in range(HOURS_DEV)], axis=1)
    station = jnp.concatenate([stations[h : h + 1, :] for h in range(HOURS_DEV)], axis=1)
    passed = jnp.concatenate([quality[h : h + 1, :] for h in range(HOURS_DEV)], axis=1)
    key = (block + hour_row * STA).astype(jnp.float32)
    from_row = lax.broadcasted_iota(jnp.int32, (count, count), 0)
    to_row = lax.broadcasted_iota(jnp.int32, (count, count), 1)
    key_col = jnp.sum(jnp.where(from_row == to_row, key, 0.0), axis=1, keepdims=True)
    earlier = (from_row < to_row) & (key_col == key)
    rank = jnp.sum(jnp.where(earlier, 1.0, 0.0), axis=0, keepdims=True).astype(jnp.int32)
    target = ((block // 4) * 2 + block % 2) * 16 + hour_row * 4 + ((block // 2) % 2) * 2 + rank
    target = jnp.where(passed > 0, target, -1)
    chosen = lax.broadcasted_iota(jnp.int32, (PLANE * 16, count), 0) == target
    tags = jnp.sum(jnp.where(chosen, (station + 1).astype(jnp.float32), 0.0), axis=1, keepdims=True)
    tag_s[...] = jnp.broadcast_to(tags, (PLANE * 16, LANES)).astype(jnp.bfloat16).reshape(tag_s.shape)
    placing = jnp.where(chosen, 1.0, 0.0).astype(jnp.bfloat16)

    pl.semaphore_wait(barrier, len(greeted))

    def spread(source, arrived, send, recv):
        for offset in OFFSETS:
            device, place = plane_peer(offset)
            remote(source.at[place], arrived.at[slot], send, recv, device).start()
        pltpu.make_async_copy(source.at[slot], arrived.at[slot], recv).start()

    spread(tag_s, tag_r, t_send, t_recv)
    for p in range(PIECES):
        for half in range(2):
            lanes = pl.ds(half * BINS + p * PB, PB)
            packed = jnp.dot(placing, rec[:, lanes], preferred_element_type=jnp.float32)
            sbuf[p, :, :, half * PB : (half + 1) * PB] = packed.astype(jnp.bfloat16).reshape(PLANE, 16, PB)
        spread(sbuf.at[p], rbuf.at[p], b_send.at[p], b_recv.at[p])

    def weigh(p):
        @pl.loop(0, PB // 32)
        def _(i):
            u = p * (PB // 32) + i
            row = pl.multiple_of(i * 32, 32)
            for n in range(LAGS // 512):
                lanes = pl.ds(n * 512, 512)
                cu, su = cos_u[pl.ds(u, 1), lanes], sin_u[pl.ds(u, 1), lanes]
                cv, sv = cos_v[:, lanes], sin_v[:, lanes]
                table[p, pl.ds(row, 32), lanes] = (cu * cv - su * sv).astype(jnp.bfloat16)
                table[p, pl.ds(PB + row, 32), lanes] = (-(su * cv) - cu * sv).astype(jnp.bfloat16)

    for p in range(PIECES):
        weigh(p)

    pltpu.make_async_copy(tag_r, tag_r, t_recv).wait()
    label = tag_r[...].astype(jnp.float32).astype(jnp.int32).reshape(PLANE * 16, LANES) - 1
    row_id = lax.broadcasted_iota(jnp.int32, (PLANE * 16, LANES), 0)
    member = ((row_id // 2 + zh) % 2) * 128 + (label // 8) * 32 + ((row_id // 4) % 4) * 8 + label % 8
    member = jnp.where(label >= 0, member, -1)
    lane_id = lax.broadcasted_iota(jnp.int32, (PLANE * 16, LANES), 1)
    for half in range(2):
        hit = jnp.where(member == lane_id + half * LANES, 1.0, 0.0)
        assign[half * LANES : (half + 1) * LANES, :] = hit.T.astype(jnp.bfloat16)
    for p in range(PIECES):
        pltpu.make_async_copy(rbuf.at[p], rbuf.at[p], b_recv.at[p]).wait()
        sums = jnp.dot(assign[...], rbuf[p].reshape(PLANE * 16, PW), preferred_element_type=jnp.float32)
        psum[p] = sums[:128]
        zsend[p] = sums[128:].astype(jnp.bfloat16)
        remote(zsend.at[p], zrecv.at[p], z_send.at[p], z_recv.at[p], z_peer).start()

    def magnitude(p):
        pltpu.make_async_copy(zrecv.at[p], zrecv.at[p], z_recv.at[p]).wait()
        summed = psum[p] + zrecv[p].astype(jnp.float32)
        psum[p] = summed
        re, im = summed[:, :PB], summed[:, PB:]
        mag = jnp.sqrt(re * re + im * im)
        high = mag.astype(jnp.bfloat16)
        mag_hi[p] = high
        mag_lo[p] = (mag - high.astype(jnp.float32)).astype(jnp.bfloat16)

    band_k = lax.broadcasted_iota(jnp.int32, (PW, PB), 0) - LANES
    band_n = lax.broadcasted_iota(jnp.int32, (PW, PB), 1)
    band = jnp.where(jnp.abs(band_k - band_n) <= SMOOTH, 1.0, 0.0).astype(jnp.bfloat16)

    def whiten(p):
        last, following = (p - 1) % PIECES, (p + 1) % PIECES
        level = jnp.zeros((128, PB), jnp.float32)
        for mag in (mag_hi, mag_lo):
            around = jnp.concatenate([mag[last, :, PB - LANES :], mag[p], mag[following, :, :LANES]], axis=1)
            level += jnp.dot(around, band, preferred_element_type=jnp.float32)
        inverse = 1.0 / (level * (1.0 / (2 * SMOOTH + 1)) + EPSILON)
        gath[p, win] = (psum[p] * jnp.concatenate([inverse, inverse], axis=1)).astype(jnp.bfloat16)

    def hand_on(p, source, way):
        item = gath.at[p, source]
        return remote(item, item, g_send.at[p, source, way], g_recv.at[p, source], (sta, win + 1 - 2 * way))

    def serve(p, source):
        for i in range(2):
            w2 = jnp.where(win == 0, 2 + i, i)
            octet = gath.at[p, source, pl.ds(pl.multiple_of(w2 * 32, 32), 32)]
            remote(octet, part.at[p, 1, source], c_send.at[p], c_recv.at[p], ((sta + 2) % STA, w2)).start()

    def begin(p):
        @pl.when(win < WIN - 1)
        def _():
            hand_on(p, win, 0).start()

        @pl.when(win > 0)
        def _():
            hand_on(p, win, 1).start()

        @pl.when((win == 0) | (win == WIN - 1))
        def _():
            serve(p, win)

    def relay(p, d):
        for way in range(2):
            source = win - d if way == 0 else win + d

            @pl.when((source >= 0) & (source < WIN))
            def _(source=source, way=way):
                item = gath.at[p, source]
                pltpu.make_async_copy(item, item, g_recv.at[p, source]).wait()
                last = win == (WIN - 1 if way == 0 else 0)

                @pl.when(jnp.logical_not(last))
                def _():
                    hand_on(p, source, way).start()

                @pl.when(last)
                def _():
                    serve(p, source)

    def swap_own(p):
        @pl.when(core == 0)
        def _():
            octet = gath.at[p, :, pl.ds(pl.multiple_of(win * 32, 32), 32)]
            remote(octet, part.at[p, 0], x_send.at[p], x_recv.at[p], other_core).start()

    def swap(p):
        @pl.when(core == 1)
        def _():
            pltpu.make_async_copy(part.at[p, 1], part.at[p, 1], c_recv.at[p]).wait()
            remote(part.at[p, 1], part.at[p, 0], x_send.at[p], x_recv.at[p], other_core).start()

    def finish(p, first, last):
        @pl.when(core == 0)
        def _():
            pltpu.make_async_copy(part.at[p, 1], part.at[p, 1], c_recv.at[p]).wait()

        pltpu.make_async_copy(part.at[p, 0], part.at[p, 0], x_recv.at[p]).wait()
        part32[...] = part[p].astype(jnp.float32)

        @pl.loop(0, PB // LANES)
        def _(t):
            re = pl.ds(pl.multiple_of(t * LANES, LANES), LANES)
            im = pl.ds(pl.multiple_of(PB + t * LANES, LANES), LANES)
            for g in range(4):
                r = g // 2
                sums = [[[jnp.zeros((8, LANES), jnp.float32) for _ in range(3)] for _ in range(4)] for _ in range(4)]
                for w2 in range(WIN):
                    for pair in range(2):
                        own = []
                        for octet in range(4):
                            at = pl.ds(octet * 32 + pair * 16, 16)
                            a, c = gath[p, w2, at, re].astype(jnp.float32), gath[p, w2, at, im].astype(jnp.float32)
                            own.append((a, c, a + c))
                        for e in range(2):
                            for jj in range(4):
                                row = (pair * 2 + e) * 8 + (g % 2) * 4 + jj
                                pr = jnp.broadcast_to(part32[r, w2, row : row + 1, re], (8, LANES))
                                pi = jnp.broadcast_to(part32[r, w2, row : row + 1, im], (8, LANES))
                                pd = pr - pi
                                for octet in range(4):
                                    a, c, ac = (v[e * 8 : e * 8 + 8] for v in own[octet])
                                    three = sums[jj][octet]
                                    three[0] = three[0] + pr * a
                                    three[1] = three[1] + pi * c
                                    three[2] = three[2] + pd * ac
                for jj in range(4):
                    at = pl.ds((r * 8 + (g % 2) * 4 + jj) * 32, 32)
                    for half, lanes in enumerate((re, im)):
                        tile = jnp.concatenate(
                            [s[2] - s[0] + s[1] if half else s[0] + s[1] for s in sums[jj]], axis=0
                        )
                        stack[at, lanes] = tile.astype(jnp.bfloat16)

        @pl.loop(0, LAGS // 512)
        def _(n):
            lanes = pl.ds(pl.multiple_of(n * 512, 512), 512)
            more = jnp.dot(stack[...], table[p, :, lanes], preferred_element_type=jnp.float32)
            if last:
                out[:, :, :, lanes] = (acc[:, lanes] + more).astype(jnp.bfloat16).reshape(ROUNDS, 8, 32, 512)
            elif first:
                acc[:, lanes] = more
            else:
                acc[:, lanes] += more

    order = (1, 2, 3, 0)
    for p in range(3):
        magnitude(p)
    for t in range(PIECES + 4):
        if t < PIECES:
            if t == 1:
                magnitude(3)
            whiten(order[t])
            begin(order[t])
        for d in (3, 2, 1):
            if 0 <= t - d < PIECES:
                relay(order[t - d], d)
                if d == 3:
                    swap_own(order[t - d])
        if t >= 4:
            finish(order[t - 4], t == 4, t == PIECES + 3)
        if 0 <= t - 3 < PIECES:
            swap(order[t - 3])

    def gone(like, semaphore):
        pltpu.make_async_copy(like, like, semaphore).wait()

    gone(tag_s.at[pl.ds(0, PLANE - 1)], t_send)
    for p in range(PIECES):
        gone(sbuf.at[p, pl.ds(0, PLANE - 1)], b_send.at[p])
        gone(zsend.at[p], z_send.at[p])
        gone(part.at[p, 0], x_send.at[p])

        @pl.when((win == 0) | (win == WIN - 1))
        def _():
            gone(part.at[p], c_send.at[p])

        for d in range(WIN):
            for way in range(2):
                source = win - d if way == 0 else win + d
                more = (source >= 0) & (source < WIN) & (win != (WIN - 1 if way == 0 else 0))

                @pl.when(more)
                def _(source=source, way=way):
                    gone(gath.at[p, source], g_send.at[p, source, way])


def hand_over(src, dst, held, came, left):
    places = [(r, pl.ds(j, 2)) for r in range(ROUNDS) for j in range(0, 8, 2)]
    into = [pltpu.make_async_copy(src.at[at], held.at[at], came.at[i]) for i, at in enumerate(places)]
    onto = [pltpu.make_async_copy(held.at[at], dst.at[at], left.at[i]) for i, at in enumerate(places)]
    for copy in into:
        copy.start()
    for before, after in zip(into, onto):
        before.wait()
        after.start()
    for copy in onto:
        copy.wait()


def angles(multiples):
    turns = np.outer(multiples, np.arange(LAGS) - LAGS // 2) % (4 * BINS)
    return turns * (2.0 * math.pi / (4 * BINS))


def shards(records, record_block, record_station, quality):
    hours, count, wide = records.shape
    scaling = 1.0 / math.sqrt(2.0 * BINS * hours * WIN)
    coarse, fine = angles(np.arange(BINS // 32) * 32 + 1), angles(np.arange(32))
    cos_u, sin_u = jnp.asarray(np.cos(coarse) * scaling, jnp.float32), jnp.asarray(np.sin(coarse) * scaling, jnp.float32)
    cos_v, sin_v = jnp.asarray(np.cos(fine), jnp.float32), jnp.asarray(np.sin(fine), jnp.float32)
    vmem = pl.BlockSpec(memory_space=pltpu.VMEM)
    dma = pltpu.SemaphoreType.DMA
    bf16, f32 = jnp.bfloat16, jnp.float32
    result = pl.pallas_call(
        kernel,
        out_shape=jax.ShapeDtypeStruct((ROUNDS, 8, 32, LAGS), bf16),
        in_specs=[vmem] * 8,
        out_specs=vmem,
        scratch_shapes=[
            pltpu.VMEM((PIECES, PLANE, 16, PW), bf16),
            pltpu.VMEM((PIECES, PLANE, 16, PW), bf16),
            pltpu.VMEM((PLANE, 16, LANES), bf16),
            pltpu.VMEM((PLANE, 16, LANES), bf16),
            pltpu.VMEM((256, PLANE * 16), bf16),
            pltpu.VMEM((PIECES, 128, PW), f32),
            pltpu.VMEM((PIECES, 128, PW), bf16),
            pltpu.VMEM((PIECES, 128, PW), bf16),
            pltpu.VMEM((PIECES, 128, PB), bf16),
            pltpu.VMEM((PIECES, 128, PB), bf16),
            pltpu.VMEM((PIECES, WIN, 128, PW), bf16),
            pltpu.VMEM((PIECES, ROUNDS, WIN, 32, PW), bf16),
            pltpu.VMEM((ROUNDS, WIN, 32, PW), f32),
            pltpu.VMEM((PIECES, PW, LAGS), bf16),
            pltpu.VMEM((512, PW), bf16),
            pltpu.VMEM((512, LAGS), f32),
            dma((PIECES,)), dma((PIECES,)), dma, dma,
            dma((PIECES,)), dma((PIECES,)), dma((PIECES, WIN, 2)), dma((PIECES, WIN)),
            dma((PIECES,)), dma((PIECES,)), dma((PIECES,)), dma((PIECES,)),
        ],
        compiler_params=pltpu.CompilerParams(
            collective_id=0, has_side_effects=True, vmem_limit_bytes=56 * 2**20
        ),
        name="correlate",
    )(record_block.reshape(hours, 1, count), record_station, quality, records.reshape(hours * count, wide), cos_u, sin_u, cos_v, sin_v)
    anywhere = pl.BlockSpec(memory_space=pl.ANY)
    return pl.pallas_call(
        hand_over,
        out_shape=jax.ShapeDtypeStruct(result.shape, result.dtype),
        in_specs=[anywhere],
        out_specs=anywhere,
        scratch_shapes=[pltpu.VMEM(result.shape, bf16), dma((8,)), dma((8,))],
        name="hand_over",
    )(result)


def solution(mesh):
    in_specs = (P("win", "sta", None), P("win", "sta", None), P("win", "sta"), P("win", "sta"))
    out_specs = P(None, "win", "sta", None)
    return jax.shard_map(shards, mesh=mesh, in_specs=in_specs, out_specs=out_specs, check_vma=False)
```
